512 devices in a mesh: ctx: 16 (over y, x_hi), cand: 8 (over z), head: 4 (over x_lo, core).
Axes of the slice: x: 4 (x_hi: 2, x_lo: 2; x = x_hi * 2 + x_lo), y: 8, z: 8, core: 2. Of those that a mesh axis runs over, the one named last changes fastest.
Arguments:
- query: bfloat16 [8, 256, 8192], P('cand', ('ctx', 'head')), may hold values from -12 to 12
- prefix_keys: bfloat16 [32768, 1024], P(('ctx', 'cand'), 'head'), may hold values from -12 to 12
- prefix_value_cache: bfloat16 [32768, 1024], P(('ctx', 'cand'), 'head'), may hold values from -6 to 6
- cont_keys: bfloat16 [8, 256, 1024], P('cand', ('ctx', 'head')), may hold values from -12 to 12
- continuation_values: bfloat16 [8, 256, 1024], P('cand', ('ctx', 'head')), may hold values from -6 to 6
- cont_lengths: int32 [8, 8], P('cand'), may hold values from 1 to 128, 256 in all within a row
Outputs:
- attended: bfloat16 [8, 256, 8192], P('cand', ('ctx', 'head'))
The draws below stay inside these ranges and needn't reach their ends.
Inputs may be any that keep to these rules, and one draw needn't show every extreme that they name: `cont_lengths`: each row sums to 256; its largest entry is 128.
All inputs are finite; a program needn't handle non-finite values.
Results may differ from the reference program's by a relative error of at most 0.0055.
Values may be sent and summed in bfloat16 or wider, within the bound.
A program may use at most 64 MiB of HBM per device.

```python
import math
import jax
import jax.numpy as jnp
import numpy as np
from jax import lax

QUERY_HEADS = 64
KEY_VALUE_HEADS = 8
HEAD_SIZE = 128
CANDS = 8
GROUP_COUNT = 8
GROUP_TOKENS = 256
PREFIX_LENGTH = 32768


def shared_parts(key):
    common_prefix = jax.random.normal(jax.random.fold_in(key, 71), (KEY_VALUE_HEADS, HEAD_SIZE), jnp.float32)
    return common_prefix


def draw_query(key, part):
    common_prefix = shared_parts(key)
    key = jax.random.fold_in(key, 1)
    array_shape = (GROUP_COUNT, GROUP_TOKENS, KEY_VALUE_HEADS, QUERY_HEADS // KEY_VALUE_HEADS, HEAD_SIZE)
    lifted = 0.49 * common_prefix[None, None, :, None, :]
    noise = jax.random.normal(jax.random.fold_in(key, 11), array_shape, jnp.float32)
    value_rows = 3.0 * (noise + lifted)
    value_rows = jnp.clip(value_rows, -12.0, 12.0)
    return value_rows.reshape(GROUP_COUNT, GROUP_TOKENS, QUERY_HEADS * HEAD_SIZE).astype(jnp.bfloat16)


def draw_prefix_keys(key, part):
    key = jax.random.fold_in(key, 2)
    array_shape = (PREFIX_LENGTH, KEY_VALUE_HEADS, HEAD_SIZE)
    value_rows = jax.random.normal(jax.random.fold_in(key, 21), array_shape, jnp.float32)
    value_rows = jnp.clip(value_rows, -12.0, 12.0)
    return value_rows.reshape(PREFIX_LENGTH, KEY_VALUE_HEADS * HEAD_SIZE).astype(jnp.bfloat16)


def draw_cont_keys(key, part):
    common_prefix = shared_parts(key)
    key = jax.random.fold_in(key, 3)
    array_shape = (GROUP_COUNT, GROUP_TOKENS, KEY_VALUE_HEADS, HEAD_SIZE)
    noise = jax.random.normal(jax.random.fold_in(key, 31), array_shape, jnp.float32)
    value_rows = jnp.clip(noise + 0.49 * common_prefix[None, None], -12.0, 12.0)
    return value_rows.reshape(GROUP_COUNT, GROUP_TOKENS, KEY_VALUE_HEADS * HEAD_SIZE).astype(jnp.bfloat16)


def level_of(stream_key, dims, shards, low, top_value):
    def one(position, shards_of):
        draws = jax.random.uniform(jax.random.fold_in(jax.random.fold_in(stream_key, 6), position), (shards_of,), jnp.float32, low / len(shards), top_value / len(shards))
        return jnp.repeat(jnp.exp(draws), dims[position] // shards_of).reshape((-1,) + (1,) * (len(dims) - position - 1))

    level = one(*shards[0])
    for cut in shards[1:]:
        level = level * one(*cut)
    return level


def length_profile(number_of, total, limit, slope):
    weights = [(1 << 20) // math.isqrt(grade ** slope) + 1 for grade in range(2, number_of + 1)]
    rest, given = total - limit - (number_of - 1), [1] * (number_of - 1)
    while rest > 0:
        movable = [i for i in range(number_of - 1) if given[i] < limit]
        mass, budget = sum([weights[i] for i in movable]), rest
        for i in movable:
            more = min(limit - given[i], max(1, budget * weights[i] // mass), rest)
            given[i] = given[i] + more
            rest = rest - more
    return np.array([limit] + given)


def uneven(key, number_of, total, bound, skew):
    if number_of == 2:
        one = jax.random.randint(key, (), max(1, total - bound), min(bound, total - 1) + 1)
        return jnp.stack([one, total - one])
    tallies = jnp.asarray(length_profile(number_of, total, bound, skew), jnp.int32)
    couples = (number_of - 1) // 2
    source_of, sink = tallies[1:1 + 2 * couples:2], tallies[2:2 + 2 * couples:2]
    room = jnp.minimum(source_of - 1, bound - sink)
    shifted = jax.random.randint(jax.random.fold_in(key, 1), (couples,), 0, 1 << 20) % (room + 1)
    tallies = tallies.at[1:1 + 2 * couples:2].set(source_of - shifted).at[2:2 + 2 * couples:2].set(sink + shifted)
    return tallies[jax.random.permutation(jax.random.fold_in(key, 2), number_of)]


def bell_draw(own_key, shape, scale, reach, shards=(), held_as=jnp.bfloat16):
    level = level_of(own_key, shape, shards, -0.22, 0.18) if shards else 1.0
    array = jax.random.normal(own_key, shape, jnp.float32) * scale * level
    return jnp.minimum(jnp.maximum(array, -reach), reach).astype(held_as)


def setup_inputs(seed: int = 0) -> dict:
    seeds = jax.random.split(jax.random.key(seed), 7)
    return {
        "query": draw_query(jax.random.fold_in(seeds[6], 71), 0),
        "prefix_keys": draw_prefix_keys(jax.random.fold_in(seeds[6], 71), 0),
        "prefix_value_cache": bell_draw(seeds[2], (PREFIX_LENGTH, KEY_VALUE_HEADS * HEAD_SIZE), 1.0, 6.0, ((0, 128), (1, 4))),
        "cont_keys": draw_cont_keys(jax.random.fold_in(seeds[6], 71), 0),
        "continuation_values": bell_draw(seeds[4], (GROUP_COUNT, GROUP_TOKENS, KEY_VALUE_HEADS * HEAD_SIZE), 1.0, 6.0, ((0, 8), (1, 64))),
        "cont_lengths": jax.vmap(lambda own: uneven(own, CANDS, GROUP_TOKENS, GROUP_TOKENS // 2, 2))(jax.random.split(seeds[5], GROUP_COUNT)).reshape((GROUP_COUNT, CANDS)).astype(jnp.int32),
    }


NEG_FILL = -1e30


def segment_of(lengths, positions):
    ends = jnp.cumsum(lengths)
    return jnp.sum((ends[None, :] <= positions[:, None]).astype(jnp.int32), axis=1)


def reference(query, prefix_keys, prefix_value_cache, cont_keys, continuation_values, cont_lengths):
    heads_per_group = QUERY_HEADS // KEY_VALUE_HEADS
    scaling = HEAD_SIZE ** -0.5
    slots = jnp.arange(GROUP_TOKENS, dtype=jnp.int32)

    def one_group(items):
        group_query, keys_cont, values_cont, lengths = items
        segment = segment_of(lengths, slots)
        recent = (segment[:, None] == segment[None, :]) & (slots[None, :] <= slots[:, None])
        allowed = jnp.concatenate([jnp.ones((GROUP_TOKENS, PREFIX_LENGTH), dtype=bool), recent], axis=1)
        allowed = jnp.repeat(allowed, heads_per_group, axis=0)

        def single_head(head):
            q_start = (head * heads_per_group * HEAD_SIZE).astype(jnp.int32)
            k_start = (head * HEAD_SIZE).astype(jnp.int32)
            q_heads = lax.dynamic_slice_in_dim(group_query, q_start, heads_per_group * HEAD_SIZE, 1).reshape(GROUP_TOKENS * heads_per_group, HEAD_SIZE)
            k_heads = jnp.concatenate([lax.dynamic_slice_in_dim(prefix_keys, k_start, HEAD_SIZE, 1), lax.dynamic_slice_in_dim(keys_cont, k_start, HEAD_SIZE, 1)], axis=0)
            v_heads = jnp.concatenate([lax.dynamic_slice_in_dim(prefix_value_cache, k_start, HEAD_SIZE, 1), lax.dynamic_slice_in_dim(values_cont, k_start, HEAD_SIZE, 1)], axis=0)
            scores = jnp.dot(q_heads, k_heads.T, preferred_element_type=jnp.float32) * scaling
            scores = jnp.where(allowed, scores, NEG_FILL)
            largest = jnp.max(scores, axis=1, keepdims=True)
            weights = jnp.where(allowed, jnp.exp(scores - largest), 0.0)
            totals = jnp.sum(weights, axis=1, keepdims=True)
            mixed = jnp.dot(weights.astype(jnp.bfloat16), v_heads, preferred_element_type=jnp.float32) / totals
            return mixed.reshape(GROUP_TOKENS, heads_per_group * HEAD_SIZE)

        each_head_rows = lax.map(single_head, jnp.arange(KEY_VALUE_HEADS, dtype=jnp.int32))
        return jnp.transpose(each_head_rows, (1, 0, 2)).reshape(GROUP_TOKENS, QUERY_HEADS * HEAD_SIZE).astype(jnp.bfloat16)

    return lax.map(one_group, (query, cont_keys, continuation_values, cont_lengths))
```

```python
import functools
import math

import jax
import jax.numpy as jnp
from jax import lax
from jax.experimental import pallas as pl
from jax.experimental.pallas import tpu as pltpu
from jax.sharding import PartitionSpec as P

MESH = pl.DeviceIdType.MESH
BF = jnp.bfloat16
F32 = jnp.float32
HEAD_SIZE = 128
SCALE = HEAD_SIZE ** -0.5
EXP2_SCALE = SCALE * math.log2(math.e)
TILE = 256
CHUNK = TILE + 64
MASKED = -1e30


def dot_nt(a, b):
    return lax.dot_general(a, b, (((1,), (1,)), ((), ())), preferred_element_type=F32)


def lanes(parts):
    return [p[:, i : i + 128] for p in parts for i in range(0, p.shape[1], 128)]


def fold(op, parts):
    parts = list(parts)
    while len(parts) > 1:
        pairs = [op(a, b) for a, b in zip(parts[::2], parts[1::2])]
        parts = pairs + (parts[-1:] if len(parts) % 2 else [])
    return parts[0]


def advance(state, scores, values):
    top = jnp.max(fold(jnp.maximum, lanes(scores)), axis=1, keepdims=True)
    if state is None:
        top = jnp.broadcast_to(top, (top.shape[0], 128))
    else:
        old = state[0]
        top = jnp.maximum(old, top)
        fade = jnp.exp2((old - top) * EXP2_SCALE)
    weights = [
        [jnp.exp2((s - top) * EXP2_SCALE) for s in lanes([part])] for part in scores
    ]
    total = fold(jnp.add, [w for part in weights for w in part])
    mixed = fold(
        jnp.add,
        [
            jnp.dot(jnp.concatenate([w.astype(BF) for w in part], axis=1), v, preferred_element_type=F32)
            for part, v in zip(weights, values)
        ],
    )
    if state is not None:
        total = total + fade * state[1]
        mixed = mixed + fade * state[2]
    return top, total, mixed


def right_slot(s):
    return 2 * s - 1 if s else 0


def left_slot(n, s):
    return 2 * s if s < n // 2 else n - 1


def kernel(
    n, q_ref, ck_ref, cv_ref, len_ref, pk_ref, pv_ref, out_ref,
    stage, outbox, inbox, kvb, qb, top, total, mixed, ckb, cvb,
    osend, lsend, orecv, lrecv, fsend, frecv,
    own_sem, box_send, box_recv, pair_send, pair_recv, kv_send, kv_recv,
    q_send, q_recv, o_send, o_recv, l_send, l_recv, f_send, f_recv,
):
    half = n // 2
    ctx, z, head = lax.axis_index("ctx"), lax.axis_index("cand"), lax.axis_index("head")
    y, xh, core = ctx // 2, ctx % 2, head % 2
    me = xh * 4 + head
    kv_head = 2 * head + xh
    u = z + core * (y - z)
    v = y + core * (z - y)

    def device(uu, vv):
        return ((vv + core * (uu - vv)) * 2 + xh, uu + core * (vv - uu), head)

    def around(a, s):
        return lax.rem(a + s + n, n)

    members = [(e // 4, e % 4) for e in range(8)]
    here = (core == 0) | (y == z)

    def source(e):
        return (v * 2 + members[e][0], u, members[e][1])

    def target(e):
        return (y * 2 + members[e][0], z, members[e][1]) if e % 2 == 0 else (z * 2 + members[e][0], y, members[e][1])

    def other(e):
        return jnp.logical_not((me == e) & here)

    barrier = pltpu.get_barrier_semaphore()

    def greet(to):
        pl.semaphore_signal(barrier, inc=1, device_id=to, device_id_type=MESH)

    for e in range(8):
        @pl.when(other(e))
        def _():
            greet(source(e))
            greet(target(e))
    partner = (y * 2 + 1 - xh, z, head)
    greet(partner)
    for s in range(1, n):
        greet(device(u, around(v, s)))
    right, left = device(around(u, 1), v), device(around(u, -1), v)
    greet(right)
    greet(left)

    own_copies = [
        pltpu.make_async_copy(
            ref.at[:, pl.ds(pl.multiple_of(xh * 128, 128), 128)], kvb.at[0, 0, i], own_sem.at[i]
        )
        for i, ref in enumerate((pk_ref, pv_ref))
    ]
    for c in own_copies:
        c.start()

    ends, so_far = [], 0
    for c in range(8):
        so_far = so_far + len_ref[0, c]
        ends.append(so_far)
    place = lax.broadcasted_iota(jnp.int32, (8, 128), 1) + 128 * lax.broadcasted_iota(jnp.int32, (8, 128), 0)
    segment = fold(jnp.add, [jnp.where(end <= place, 1.0, 0.0) for end in ends])
    for k in range(8):
        for j in range(8):
            stage[k, j * 4 : j * 4 + 4, :] = q_ref[0, :, (k * 8 + j) * 128 : (k * 8 + j + 1) * 128].astype(F32)
        stage[k, 32:36, :] = ck_ref[0, :, k * 128 : k * 128 + 128].astype(F32)
        stage[k, 36:40, :] = cv_ref[0, :, k * 128 : k * 128 + 128].astype(F32)
        stage[k, 40:48, :] = segment
        outbox[k] = stage[k].astype(BF)

    pl.semaphore_wait(barrier, 1 + (n - 1) + 2 + 16 - 2 * here.astype(jnp.int32))

    def remote(src, dst, send, recv, to):
        return pltpu.make_async_remote_copy(
            src_ref=src, dst_ref=dst, send_sem=send, recv_sem=recv, device_id=to, device_id_type=MESH
        )

    pair = [
        remote(
            ref.at[:, pl.ds(pl.multiple_of((1 - xh) * 128, 128), 128)],
            kvb.at[0, 1, i], pair_send.at[i], pair_recv.at[i], partner,
        )
        for i, ref in enumerate((pk_ref, pv_ref))
    ]
    for c in pair:
        c.start()

    def box(e):
        k = 2 * members[e][1] + members[e][0]
        return remote(outbox.at[k], inbox.at[me], box_send.at[e], box_recv.at[me], target(e))

    def box_in(e):
        return remote(outbox.at[0], inbox.at[e], box_send.at[e], box_recv.at[e], source(e))

    for e in range(8):
        @pl.when(other(e))
        def _():
            box(e).start()

        @pl.when(jnp.logical_not(other(e)))
        def _():
            inbox[e] = outbox[kv_head]

    def kv_copies(s, sub):
        rs, ls = right_slot(s), left_slot(n, s)
        out = []
        if s < half or sub == 0:
            out.append(remote(kvb.at[right_slot(s - 1), sub], kvb.at[rs, sub], kv_send.at[rs, sub], kv_recv.at[rs, sub], right))
        if s < half or sub == 1:
            out.append(remote(kvb.at[left_slot(n, s - 1) if s > 1 else 0, sub], kvb.at[ls, sub], kv_send.at[ls, sub], kv_recv.at[ls, sub], left))
        return out

    def kv_begin(s, sub):
        if s <= half:
            for c in kv_copies(s, sub):
                c.start()

    def kv_arrive(s, sub):
        if s <= half:
            if s == half:
                for c in kv_copies(s, sub):
                    c.wait_recv()
                return
            copies, nexts = kv_copies(s, sub), (kv_copies(s + 1, sub))
            copies[0].wait_recv()
            copies[1].wait_recv()
            for c in nexts:
                c.start()

    for c in own_copies:
        c.wait()
    kv_begin(1, 0)

    q_right, q_left = device(u, around(v, 1)), device(u, around(v, -1))

    def q_copies(s):
        rs, ls = right_slot(s), left_slot(n, s)
        first, second = (pl.ds(0, CHUNK), pl.ds(0, CHUNK)) if s < half else (pl.ds(0, CHUNK // 2), pl.ds(CHUNK // 2, CHUNK // 2))
        return [
            remote(qb.at[right_slot(s - 1), first], qb.at[rs, first], q_send.at[0, s - 1], q_recv.at[0, s - 1], q_right),
            remote(qb.at[left_slot(n, s - 1) if s > 1 else 0, second], qb.at[ls, second], q_send.at[1, s - 1], q_recv.at[1, s - 1], q_left),
        ]

    for e in range(8):
        @pl.when(other(e))
        def _():
            box_in(e).wait_recv()
    for e in range(8):
        qb[0, e * 32 : e * 32 + 32, :] = inbox[e, 0:32, :]
        extra = inbox[e, 32:48, :].astype(F32)
        stage[0, e * 4 : e * 4 + 4, :] = extra[0:4]
        stage[1, e * 4 : e * 4 + 4, :] = extra[4:8]
    qb[0, TILE : TILE + 32, :] = stage[0, 0:32, :].astype(BF)
    qb[0, TILE + 32 : TILE + 64, :] = stage[1, 0:32, :].astype(BF)
    for c in q_copies(1):
        c.start()
    for c in pair:
        c.wait_recv()
    kv_begin(1, 1)

    def store(r, state):
        top[r], total[r], mixed[r] = state

    def update(r, slots, first=False):
        q = qb[r, 0:TILE, :]
        pieces = [(s, ab) for s in slots for ab in (0, 1)]
        scores = [dot_nt(q, kvb[s, ab, 0]) for s, ab in pieces]
        values = [kvb[s, ab, 1] for s, ab in pieces]
        return advance(None if first else (top[r], total[r], mixed[r]), scores, values)

    def sweep(low, high, slots, first=False):
        def one(r, _):
            store(r, update(r, slots, first))
            return 0

        lax.fori_loop(low, high, one, 0)

    sweep(0, 1, (0,), True)
    for s in range(1, half + 1):
        kv_arrive((s + 1) // 2, (s + 1) % 2)
        copies = q_copies(s)
        for c in copies:
            c.wait_recv()
        if s < half:
            for c in q_copies(s + 1):
                c.start()
        sweep(2 * s - 1, min(2 * s + 1, n), (0,), True)
    arrived = [((s + 1) // 2, (s + 1) % 2) for s in range(1, half + 1)]
    waiting = [(s, sub) for s in range(1, half + 1) for sub in (0, 1) if (s, sub) not in arrived]

    def arrive_until(s, sub):
        while waiting and waiting[0] <= (s, sub):
            kv_arrive(*waiting.pop(0))

    for r in range(n):
        d = -((r + 1) // 2) if r % 2 or r == n - 1 else r // 2
        at = pl.ds(pl.multiple_of(around(v, d) * 32, 32), 32)
        ckb[at, :] = qb[r, TILE : TILE + 32, :]
        cvb[at, :] = qb[r, TILE + 32 : TILE + 64, :]
    wide = min(128, 32 * n)
    marks = inbox[0, 32:48, :].astype(F32)
    row = lax.broadcasted_iota(jnp.int32, (TILE, wide), 0)
    slot = v * 32 + (row // 32) * 4 + row % 4
    lane = lax.broadcasted_iota(jnp.int32, (TILE, wide), 1)
    halves = range(32 * n // wide)
    own = fold(jnp.add, [
        jnp.sum(jnp.where(lane + h * wide == slot, marks[8 + h : 9 + h, :wide], 0.0), axis=1, keepdims=True) for h in halves
    ])
    scores = []
    for h in halves:
        allowed = (marks[8 + h : 9 + h, :wide] == own) & (lane + h * wide <= slot)
        scores.append(jnp.where(allowed, dot_nt(qb[0, 0:TILE, :], ckb[h * wide : (h + 1) * wide, :]), MASKED))
    store(0, advance((top[0], total[0], mixed[0]), scores, [cvb[h * wide : (h + 1) * wide, :] for h in halves]))

    for s in range(1, half):
        arrive_until(s, 1)
        slots = (right_slot(s), left_slot(n, s))
        sweep(0, n // 2, slots)
        arrive_until(s + 1, 0)
        sweep(n // 2, n, slots)
    arrive_until(half, 1)

    row = lax.broadcasted_iota(jnp.int32, (128, 128), 0)
    lane = lax.broadcasted_iota(jnp.int32, (128, 128), 1)
    diagonal = row == lane

    def finish(r):
        t, w, m = update(r, (n - 1,))
        w = jnp.sum(w, axis=1, keepdims=True)
        lse = t * SCALE + jnp.log(w)
        for h in range(2):
            lsend[r, h : h + 1, :] = jnp.sum(
                jnp.where(diagonal, lse[h * 128 : h * 128 + 128], 0.0), axis=0, keepdims=True
            )
        return m / w

    def o_copies(r, mirror, to):
        return [
            remote(osend.at[r], orecv.at[mirror], o_send.at[r], o_recv.at[mirror], to),
            remote(lsend.at[r], lrecv.at[mirror], l_send.at[r], l_recv.at[mirror], to),
        ]

    sent = []
    for r in range(n - 1, 0, -1):
        osend[r] = finish(r).astype(BF)
        if r == n - 1:
            copies = o_copies(r, r, device(u, around(v, half)))
        elif r % 2:
            copies = o_copies(r, r + 1, device(u, around(v, -((r + 1) // 2))))
        else:
            copies = o_copies(r, r - 1, device(u, around(v, r // 2)))
        for c in copies:
            c.start()
        sent += copies
    mine = finish(0)
    for c in sent:
        c.wait_recv()
    pieces = [lsend[0, 0:2, :]] + [lrecv[r, 0:2, :] for r in range(1, n)]
    largest = fold(jnp.maximum, pieces)
    shares = [jnp.exp(p - largest) for p in pieces]
    whole = fold(jnp.add, shares)
    shares = [p / whole for p in shares]
    for h in range(2):
        rows = slice(h * 128, h * 128 + 128)
        terms = []
        for r in range(n):
            share = jnp.sum(jnp.where(diagonal, shares[r][h : h + 1, :], 0.0), axis=1, keepdims=True)
            terms.append(share * (mine[rows] if r == 0 else orecv[r, rows, :].astype(F32)))
        fsend[rows, :] = fold(jnp.add, terms).astype(BF)

    def final(e):
        return remote(fsend.at[e * 32 : e * 32 + 32], frecv.at[kv_head], f_send.at[e], f_recv.at[kv_head], source(e))

    def final_in(e):
        k = 2 * members[e][1] + members[e][0]
        return remote(fsend.at[0:32], frecv.at[k], f_send.at[e], f_recv.at[k], target(e))

    for e in range(8):
        @pl.when(other(e))
        def _():
            final(e).start()

        @pl.when(jnp.logical_not(other(e)))
        def _():
            frecv[kv_head] = fsend[e * 32 : e * 32 + 32, :]

    for c in sent + pair + [c for s in range(1, half + 1) for sub in (0, 1) for c in kv_copies(s, sub)]:
        c.wait_send()
    for s in range(1, half + 1):
        for c in q_copies(s):
            c.wait_send()
    for e in range(8):
        @pl.when(other(e))
        def _():
            box(e).wait_send()
            final(e).wait_send()
            final_in(e).wait_recv()
    out_ref[...] = frecv[...]


def per_device(n, query, prefix_keys, prefix_value_cache, cont_keys, continuation_values, cont_lengths):
    rows = prefix_keys.shape[0]
    vmem = pl.BlockSpec(memory_space=pltpu.VMEM)
    anywhere = pl.BlockSpec(memory_space=pl.ANY)
    dma = pltpu.SemaphoreType.DMA
    out = pl.pallas_call(
        functools.partial(kernel, n),
        out_shape=jax.ShapeDtypeStruct((8, 32, 128), BF),
        in_specs=[vmem, vmem, vmem, pl.BlockSpec(memory_space=pltpu.SMEM), anywhere, anywhere],
        out_specs=vmem,
        scratch_shapes=[
            pltpu.VMEM((8, 48, 128), F32),
            pltpu.VMEM((8, 48, 128), BF),
            pltpu.VMEM((8, 48, 128), BF),
            pltpu.VMEM((n, 2, 2, rows, 128), BF),
            pltpu.VMEM((n, CHUNK, 128), BF),
            pltpu.VMEM((n, TILE, 128), F32),
            pltpu.VMEM((n, TILE, 128), F32),
            pltpu.VMEM((n, TILE, 128), F32),
            pltpu.VMEM((32 * n, 128), BF),
            pltpu.VMEM((32 * n, 128), BF),
            pltpu.VMEM((n, TILE, 128), BF),
            pltpu.VMEM((n, 8, 128), F32),
            pltpu.VMEM((n, TILE, 128), BF),
            pltpu.VMEM((n, 8, 128), F32),
            pltpu.VMEM((TILE, 128), BF),
            pltpu.VMEM((8, 32, 128), BF),
            dma((2,)), dma((8,)), dma((8,)), dma((2,)), dma((2,)), dma((n, 2)), dma((n, 2)),
            dma((2, n // 2)), dma((2, n // 2)), dma((n,)), dma((n,)), dma((n,)), dma((n,)), dma((8,)), dma((8,)),
        ],
        compiler_params=pltpu.CompilerParams(
            collective_id=0, has_side_effects=True, vmem_limit_bytes=48 * 1024 * 1024
        ),
        cost_estimate=pl.CostEstimate(flops=4_300_000_000, bytes_accessed=1_000_000, transcendentals=8_400_000),
    )(query, cont_keys, continuation_values, cont_lengths, prefix_keys, prefix_value_cache)
    return jnp.transpose(out.reshape(8, 8, 4, 128), (2, 0, 1, 3)).reshape(query.shape)


def solution(mesh):
    n = mesh.shape["cand"]
    return jax.shard_map(
        functools.partial(per_device, n),
        mesh=mesh,
        in_specs=(
            P("cand", ("ctx", "head"), None),
            P(("ctx", "cand"), "head"),
            P(("ctx", "cand"), "head"),
            P("cand", ("ctx", "head"), None),
            P("cand", ("ctx", "head"), None),
            P("cand", None),
        ),
        out_specs=P("cand", ("ctx", "head"), None),
        check_vma=False,
    )
```

```python
import functools
import math

import jax
import jax.numpy as jnp
from jax import lax
from jax.experimental import pallas as pl
from jax.experimental.pallas import tpu as pltpu
from jax.sharding import PartitionSpec as P

MESH = pl.DeviceIdType.MESH
BF = jnp.bfloat16
F32 = jnp.float32
HEAD_SIZE = 128
SCALE = HEAD_SIZE ** -0.5
EXP2_SCALE = SCALE * math.log2(math.e)
TILE = 256
CHUNK = TILE + 64
MASKED = -1e30


def dot_nt(a, b):
    return lax.dot_general(a, b, (((1,), (1,)), ((), ())), preferred_element_type=F32)


def lanes(parts):
    return [p[:, i : i + 128] for p in parts for i in range(0, p.shape[1], 128)]


def fold(op, parts):
    parts = list(parts)
    while len(parts) > 1:
        pairs = [op(a, b) for a, b in zip(parts[::2], parts[1::2])]
        parts = pairs + (parts[-1:] if len(parts) % 2 else [])
    return parts[0]


def advance(state, scores, values):
    top = jnp.max(fold(jnp.maximum, lanes(scores)), axis=1, keepdims=True)
    if state is None:
        top = jnp.broadcast_to(top, (top.shape[0], 128))
    else:
        old = state[0]
        top = jnp.maximum(old, top)
        fade = jnp.exp2((old - top) * EXP2_SCALE)
    weights = [
        [jnp.exp2((s - top) * EXP2_SCALE) for s in lanes([part])] for part in scores
    ]
    total = fold(jnp.add, [w for part in weights for w in part])
    mixed = fold(
        jnp.add,
        [
            jnp.dot(jnp.concatenate([w.astype(BF) for w in part], axis=1), v, preferred_element_type=F32)
            for part, v in zip(weights, values)
        ],
    )
    if state is not None:
        total = total + fade * state[1]
        mixed = mixed + fade * state[2]
    return top, total, mixed


def right_slot(s):
    return 2 * s - 1 if s else 0


def left_slot(n, s):
    return 2 * s if s < n // 2 else n - 1


ORDER = ("10", "11", "X0", "X1", "S", "20", "21", "12", "13", "N",)
UNITS = {0: ("22", "23",), 1: ("30", "31",), 2: ("32", "33",), 3: ("F",), 5: ("40", "41", "42", "43",)}
FIRST = 3


def kernel(
    n, q_hbm, ck_hbm, cv_hbm, len_hbm, pk_ref, pv_ref, out_ref,
    ck_ref, cv_ref, len_ref,
    stage, outbox, inbox, kvb, others, qb, top, total, mixed, ckb, cvb,
    osend, lsend, orecv, lrecv, fsend, frecv,
    own_sem, box_send, box_recv, pair_send, pair_recv, kv_send, kv_recv,
    q_send, q_recv, o_send, o_recv, l_send, l_recv, f_send, f_recv,
):
    half, near = n // 2, n // 4
    ctx, z, head = lax.axis_index("ctx"), lax.axis_index("cand"), lax.axis_index("head")
    y, xh, core = ctx // 2, ctx % 2, head % 2
    me = xh * 4 + head
    kv_head = 2 * head + xh

    def around(a, s):
        return lax.rem(a + s + n, n)

    u = z + core * (y - z)
    v = y + core * (around(z, -half) - y)

    def device(uu, vv):
        return ((vv + core * (uu - vv)) * 2 + xh, uu + core * (around(vv, half) - uu), head)

    members = [(e // 4, e % 4) for e in range(8)]
    here = core == 0

    def source(e):
        return (v * 2 + members[e][0], u, members[e][1])

    def target(e):
        return (y * 2 + members[e][0], z, members[e][1]) if e % 2 == 0 else (z * 2 + members[e][0], around(y, half), members[e][1])

    def other(e):
        return jnp.logical_not((me == e) & here)

    loads = [
        pltpu.make_async_copy(src, dst, own_sem.at[2 + i])
        for i, (src, dst) in enumerate(((q_hbm, outbox.at[:, 0:32]), (ck_hbm, ck_ref), (cv_hbm, cv_ref), (len_hbm, len_ref)))
    ]
    own_copies = [
        pltpu.make_async_copy(
            ref.at[:, pl.ds(pl.multiple_of(at * 128, 128), 128)], dst.at[i], own_sem.at[sem + i]
        )
        for at, dst, sem in ((xh, kvb.at[0, 0], 0), (1 - xh, others, 6))
        for i, ref in enumerate((pk_ref, pv_ref))
    ]
    for c in loads + own_copies:
        c.start()

    barrier = pltpu.get_barrier_semaphore()

    def greet(to):
        pl.semaphore_signal(barrier, inc=1, device_id=to, device_id_type=MESH)

    for e in range(8):
        @pl.when(other(e))
        def _():
            greet(source(e))
            greet(target(e))
    partner = (y * 2 + 1 - xh, z, head)
    greet(partner)
    for s in range(1, n):
        greet(device(u, around(v, s)))
    right, left = device(around(u, 1), v), device(around(u, -1), v)
    greet(right)
    greet(left)

    for c in loads:
        c.wait()
    ends, so_far = [], 0
    for c in range(8):
        so_far = so_far + len_ref[0, c]
        ends.append(so_far)
    place = lax.broadcasted_iota(jnp.int32, (8, 128), 1) + 128 * lax.broadcasted_iota(jnp.int32, (8, 128), 0)
    segment = fold(jnp.add, [jnp.where(end <= place, 1.0, 0.0) for end in ends])
    cks, cvs = ck_ref[...].astype(F32), cv_ref[...].astype(F32)
    for k in range(8):
        stage[0:4] = cks[k * 4 : k * 4 + 4]
        stage[4:8] = cvs[k * 4 : k * 4 + 4]
        stage[8:16] = segment
        outbox[k, 32:48, :] = stage[0:16].astype(BF)

    pl.semaphore_wait(barrier, 1 + (n - 1) + 2 + 16 - 2 * here.astype(jnp.int32))

    def remote(src, dst, send, recv, to):
        return pltpu.make_async_remote_copy(
            src_ref=src, dst_ref=dst, send_sem=send, recv_sem=recv, device_id=to, device_id_type=MESH
        )

    def box(e):
        k = 2 * members[e][1] + members[e][0]
        return remote(outbox.at[k], inbox.at[me], box_send.at[e], box_recv.at[me], target(e))

    def box_in(e):
        return remote(outbox.at[0], inbox.at[e], box_send.at[e], box_recv.at[e], source(e))

    for e in range(8):
        @pl.when(other(e))
        def _():
            box(e).start()

        @pl.when(jnp.logical_not(other(e)))
        def _():
            inbox[e] = outbox[kv_head]
    crossing = [remote(others.at[i], kvb.at[0, 1, i], pair_send.at[i], pair_recv.at[i], partner) for i in (0, 1)]

    def kv_copies(s, piece):
        out = []
        sub, i = piece // 2, piece % 2
        for sign, slot, to in ((1, right_slot, right), (-1, functools.partial(left_slot, n), left)):
            if s == half and sub == (sign > 0):
                continue
            src, dst = slot(s - 1) if s > 1 else 0, slot(s)
            out.append(remote(kvb.at[src, sub, i], kvb.at[dst, sub, i], kv_send.at[dst, piece], kv_recv.at[dst, piece], to))
        return out

    def kv_do(s, piece, act):
        if s <= half:
            for c in kv_copies(s, piece):
                act(c)

    def kv_event(s, piece):
        kv_do(s, piece, lambda c: c.wait_recv())
        if s < half:
            kv_do(s + 1, piece, lambda c: c.start())

    for c in own_copies[2:]:
        c.wait()
    for c in crossing:
        c.start()

    for i in (0, 1):
        own_copies[i].wait()
        kv_do(1, i, lambda c: c.start())

    def q_copies(far):
        out = []
        for s in range(1, near + 1):
            for sign, slot in ((1, right_slot), (-1, functools.partial(left_slot, n))):
                src, dst = (slot(near), slot(near + s)) if far else (0, slot(s))
                last = near + s == half
                rows = pl.ds(0, CHUNK)
                if far and last:
                    rows = pl.ds(0 if sign > 0 else CHUNK // 2, CHUNK // 2)
                sem = n if far and last and sign < 0 else dst
                out.append(remote(
                    qb.at[src, rows], qb.at[dst, rows], q_send.at[sem], q_recv.at[sem], device(u, around(v, sign * s))
                ))
        return out

    def q_do(far, act):
        for c in q_copies(far):
            act(c)

    def scattered():
        for e in range(8):
            @pl.when(other(e))
            def _():
                box_in(e).wait_recv()
        for e in range(8):
            qb[0, e * 32 : e * 32 + 32, :] = inbox[e, 0:32, :]
            extra = inbox[e, 32:48, :].astype(F32)
            stage[e * 4 : e * 4 + 4] = extra[0:4]
            stage[32 + e * 4 : 32 + e * 4 + 4] = extra[4:8]
        qb[0, TILE : TILE + 64, :] = stage[...].astype(BF)
        q_do(False, lambda c: c.start())

    def run(order):
        for token in order:
            if token == "S":
                scattered()
            elif token == "N":
                q_do(False, lambda c: c.wait_recv())
                q_do(True, lambda c: c.start())
            elif token == "F":
                q_do(True, lambda c: c.wait_recv())
            elif token[0] == "X":
                i = int(token[1])
                crossing[i].wait_recv()
                kv_do(1, 2 + i, lambda c: c.start())
            else:
                kv_event(int(token[0]), int(token[1]))

    run(ORDER)

    def own_continuation():
        for r in range(n):
            d = -((r + 1) // 2) if r % 2 else r // 2
            at = pl.ds(pl.multiple_of(around(v, d) * 32, 32), 32)
            ckb[at, :] = qb[r, TILE : TILE + 32, :]
            cvb[at, :] = qb[r, TILE + 32 : TILE + 64, :]
        wide = min(128, 32 * n)
        marks = inbox[0, 32:48, :].astype(F32)
        row = lax.broadcasted_iota(jnp.int32, (TILE, wide), 0)
        slot = v * 32 + (row // 32) * 4 + row % 4
        lane = lax.broadcasted_iota(jnp.int32, (TILE, wide), 1)
        halves = range(32 * n // wide)
        own = fold(jnp.add, [
            jnp.sum(jnp.where(lane + h * wide == slot, marks[8 + h : 9 + h, :wide], 0.0), axis=1, keepdims=True) for h in halves
        ])
        scores = []
        for h in halves:
            allowed = (marks[8 + h : 9 + h, :wide] == own) & (lane + h * wide <= slot)
            scores.append(jnp.where(allowed, dot_nt(qb[0, 0:TILE, :], ckb[h * wide : (h + 1) * wide, :]), MASKED))
        state = (top[0], total[0], mixed[0])
        top[0], total[0], mixed[0] = advance(state, scores, [cvb[h * wide : (h + 1) * wide, :] for h in halves])

    row = lax.broadcasted_iota(jnp.int32, (128, 128), 0)
    lane = lax.broadcasted_iota(jnp.int32, (128, 128), 1)
    diagonal = row == lane

    def finish(r):
        w = jnp.sum(total[r], axis=1, keepdims=True)
        lse = top[r] * SCALE + jnp.log(w)
        for h in range(2):
            lsend[r, h : h + 1, :] = jnp.sum(
                jnp.where(diagonal, lse[h * 128 : h * 128 + 128], 0.0), axis=0, keepdims=True
            )
        return mixed[r] / w

    def o_copies(r):
        odd = r % 2
        mirror = r + 2 * odd - 1 - r // (n - 1)
        to = device(u, around(v, (1 - odd) * (r // 2) - odd * ((r + 1) // 2)))
        return [
            remote(osend.at[r], orecv.at[mirror], o_send.at[r], o_recv.at[mirror], to),
            remote(lsend.at[r], lrecv.at[mirror], l_send.at[r], l_recv.at[mirror], to),
        ]

    def give(r, _):
        osend[r] = finish(r).astype(BF)
        for c in o_copies(r):
            c.start()
        return 0

    def each_sent(act):
        def one(r, _):
            for c in o_copies(r):
                act(c)
            return 0

        lax.fori_loop(1, n, one, 0)

    pairs, tiles = n // 2, n // 2
    first = FIRST if n == 8 else 1
    before = UNITS if n == 8 else {1: ("F",)}
    top[...] = jnp.full(top.shape, MASKED, F32)
    total[...] = jnp.zeros(total.shape, F32)
    mixed[...] = jnp.zeros(mixed.shape, F32)

    def visit(i, _):
        for at, events in before.items():
            @pl.when(i == at)
            def _():
                run(events)

        second, third = (i + 2 * pairs - first) // (2 * pairs), (i + pairs - first) // (2 * pairs)
        part, p = second - third, i - first * second - (pairs - first) * third
        rows = pl.ds(part * tiles, tiles)
        q = jnp.concatenate([qb[part * tiles + r, 0:TILE, :] for r in range(tiles)], axis=0)
        pieces = [(2 * p + s, ab) for s in (0, 1) for ab in (0, 1)]
        scores = [dot_nt(q, kvb[s, ab, 0]) for s, ab in pieces]
        state = tuple(x[rows].reshape(tiles * TILE, 128) for x in (top, total, mixed))
        state = advance(state, scores, [kvb[s, ab, 1] for s, ab in pieces])
        for x, new in zip((top, total, mixed), state):
            x[rows] = new.reshape(tiles, TILE, 128)

        @pl.when(i == first + pairs - 1)
        def _():
            lax.fori_loop(tiles, n, give, 0)
            own_continuation()

        return 0

    lax.fori_loop(0, 2 * pairs, visit, 0)

    lax.fori_loop(1, tiles, give, 0)
    mine = finish(0)
    each_sent(lambda c: c.wait_recv())
    pieces = [lsend[0, 0:2, :]] + [lrecv[r, 0:2, :] for r in range(1, n)]
    largest = fold(jnp.maximum, pieces)
    shares = [jnp.exp(p - largest) for p in pieces]
    whole = fold(jnp.add, shares)
    shares = [p / whole for p in shares]
    for h in range(2):
        rows = slice(h * 128, h * 128 + 128)
        terms = []
        for r in range(n):
            share = jnp.sum(jnp.where(diagonal, shares[r][h : h + 1, :], 0.0), axis=1, keepdims=True)
            terms.append(share * (mine[rows] if r == 0 else orecv[r, rows, :].astype(F32)))
        fsend[rows, :] = fold(jnp.add, terms).astype(BF)

    def final(e):
        return remote(fsend.at[e * 32 : e * 32 + 32], frecv.at[kv_head], f_send.at[e], f_recv.at[kv_head], source(e))

    def final_in(e):
        k = 2 * members[e][1] + members[e][0]
        return remote(fsend.at[0:32], frecv.at[k], f_send.at[e], f_recv.at[k], target(e))

    for e in range(8):
        @pl.when(other(e))
        def _():
            final(e).start()

        @pl.when(jnp.logical_not(other(e)))
        def _():
            frecv[kv_head] = fsend[e * 32 : e * 32 + 32, :]

    each_sent(lambda c: c.wait_send())
    for c in crossing:
        c.wait_send()
    for s in range(1, half + 1):
        for piece in range(4):
            kv_do(s, piece, lambda c: c.wait_send())
    q_do(False, lambda c: c.wait_send())
    q_do(True, lambda c: c.wait_send())
    for e in range(8):
        @pl.when(other(e))
        def _():
            box(e).wait_send()
            final(e).wait_send()
            final_in(e).wait_recv()
    out_ref[...] = frecv[...]


def by_head(flat, heads):
    return jnp.transpose(flat.reshape(4, 8 * heads, 128), (1, 0, 2)).reshape(-1, 128)


def per_device(n, query, prefix_keys, prefix_value_cache, cont_keys, continuation_values, cont_lengths):
    rows = prefix_keys.shape[0]
    vmem = pl.BlockSpec(memory_space=pltpu.VMEM)
    anywhere = pl.BlockSpec(memory_space=pltpu.MemorySpace.HBM)
    dma = pltpu.SemaphoreType.DMA
    out = pl.pallas_call(
        functools.partial(kernel, n),
        out_shape=jax.ShapeDtypeStruct((8, 32, 128), BF),
        in_specs=[anywhere] * 6,
        out_specs=vmem,
        scratch_shapes=[
            pltpu.VMEM((32, 128), BF),
            pltpu.VMEM((32, 128), BF),
            pltpu.SMEM(cont_lengths.shape, jnp.int32),
            pltpu.VMEM((64, 128), F32),
            pltpu.VMEM((8, 48, 128), BF),
            pltpu.VMEM((8, 48, 128), BF),
            pltpu.VMEM((n, 2, 2, rows, 128), BF),
            pltpu.VMEM((2, rows, 128), BF),
            pltpu.VMEM((n, CHUNK, 128), BF),
            pltpu.VMEM((n, TILE, 128), F32),
            pltpu.VMEM((n, TILE, 128), F32),
            pltpu.VMEM((n, TILE, 128), F32),
            pltpu.VMEM((32 * n, 128), BF),
            pltpu.VMEM((32 * n, 128), BF),
            pltpu.VMEM((n, TILE, 128), BF),
            pltpu.VMEM((n, 8, 128), F32),
            pltpu.VMEM((n, TILE, 128), BF),
            pltpu.VMEM((n, 8, 128), F32),
            pltpu.VMEM((TILE, 128), BF),
            pltpu.VMEM((8, 32, 128), BF),
            dma((8,)), dma((8,)), dma((8,)), dma((2,)), dma((2,)), dma((n, 4)), dma((n, 4)),
            dma((n + 1,)), dma((n + 1,)), dma((n,)), dma((n,)), dma((n,)), dma((n,)), dma((8,)), dma((8,)),
        ],
        compiler_params=pltpu.CompilerParams(
            collective_id=0, has_side_effects=True, vmem_limit_bytes=56 * 1024 * 1024
        ),
        cost_estimate=pl.CostEstimate(flops=4_300_000_000, bytes_accessed=1_000_000, transcendentals=8_400_000),
    )(*[
        pltpu.with_memory_space_constraint(x, pltpu.MemorySpace.HBM)
        for x in (
            by_head(query, 8).reshape(8, 32, 128), by_head(cont_keys, 1), by_head(continuation_values, 1),
            cont_lengths, prefix_keys, prefix_value_cache,
        )
    ])
    return jnp.transpose(out.reshape(8, 8, 4, 128), (2, 0, 1, 3)).reshape(query.shape)


def solution(mesh):
    n = mesh.shape["cand"]
    return jax.shard_map(
        functools.partial(per_device, n),
        mesh=mesh,
        in_specs=(
            P("cand", ("ctx", "head"), None),
            P(("ctx", "cand"), "head"),
            P(("ctx", "cand"), "head"),
            P("cand", ("ctx", "head"), None),
            P("cand", ("ctx", "head"), None),
            P("cand", None),
        ),
        out_specs=P("cand", ("ctx", "head"), None),
        check_vma=False,
    )
```

```python
import functools
import math

import jax
import jax.numpy as jnp
from jax import lax
from jax.experimental import pallas as pl
from jax.experimental.pallas import tpu as pltpu
from jax.sharding import PartitionSpec as P

MESH = pl.DeviceIdType.MESH
BF = jnp.bfloat16
F32 = jnp.float32
HEAD_SIZE = 128
SCALE = HEAD_SIZE ** -0.5
EXP2_SCALE = SCALE * math.log2(math.e)
TILE = 256
CHUNK = TILE + 64
MASKED = -1e30


def dot_nt(a, b):
    return lax.dot_general(a, b, (((1,), (1,)), ((), ())), preferred_element_type=F32)


def lanes(parts):
    return [p[:, i : i + 128] for p in parts for i in range(0, p.shape[1], 128)]


def fold(op, parts):
    parts = list(parts)
    while len(parts) > 1:
        pairs = [op(a, b) for a, b in zip(parts[::2], parts[1::2])]
        parts = pairs + (parts[-1:] if len(parts) % 2 else [])
    return parts[0]


def advance(state, scores, values):
    top = jnp.max(fold(jnp.maximum, lanes(scores)), axis=1, keepdims=True)
    if state is None:
        top = jnp.broadcast_to(top, (top.shape[0], 128))
    else:
        old = state[0]
        top = jnp.maximum(old, top)
        fade = jnp.exp2((old - top) * EXP2_SCALE)
    weights = [
        [jnp.exp2((s - top) * EXP2_SCALE) for s in lanes([part])] for part in scores
    ]
    total = fold(jnp.add, [w for part in weights for w in part])
    mixed = fold(
        jnp.add,
        [
            jnp.dot(jnp.concatenate([w.astype(BF) for w in part], axis=1), v, preferred_element_type=F32)
            for part, v in zip(weights, values)
        ],
    )
    if state is not None:
        total = total + fade * state[1]
        mixed = mixed + fade * state[2]
    return top, total, mixed


def right_slot(s):
    return 2 * s - 1 if s else 0


def left_slot(n, s):
    return 2 * s if s < n // 2 else n - 1


ORDER = ("S", "10", "11", "X0", "X1", "N", "20", "21", "12", "13",)
UNITS = {1: ("30", "31",)}
FIRST = 2
FAR_UNITS = {2: ("22", "23", "40", "41",)}


def kernel(
    n, q_hbm, ck_hbm, cv_hbm, len_hbm, pk_ref, pv_ref, out_ref,
    ck_ref, cv_ref, len_ref,
    stage, outbox, inbox, kvb, others, qb, top, total, mixed, ckb, cvb,
    osend, lsend, orecv, lrecv, fsend, frecv,
    own_sem, box_send, box_recv, pair_send, pair_recv, kv_send, kv_recv,
    q_send, q_recv, o_send, o_recv, l_send, l_recv, f_send, f_recv,
):
    half, near = n // 2, n // 4
    ctx, z, head = lax.axis_index("ctx"), lax.axis_index("cand"), lax.axis_index("head")
    y, xh, core = ctx // 2, ctx % 2, head % 2
    me = xh * 4 + head
    kv_head = 2 * head + xh

    def around(a, s):
        return lax.rem(a + s + n, n)

    u = z + core * (y - z)
    v = y + core * (around(z, -half) - y)

    def device(uu, vv):
        return ((vv + core * (uu - vv)) * 2 + xh, uu + core * (around(vv, half) - uu), head)

    members = [(e // 4, e % 4) for e in range(8)]
    here = core == 0

    def source(e):
        return (v * 2 + members[e][0], u, members[e][1])

    def target(e):
        return (y * 2 + members[e][0], z, members[e][1]) if e % 2 == 0 else (z * 2 + members[e][0], around(y, half), members[e][1])

    def other(e):
        return jnp.logical_not((me == e) & here)

    loads = [
        pltpu.make_async_copy(src, dst, own_sem.at[2 + i])
        for i, (src, dst) in enumerate(((q_hbm, outbox.at[:, 0:32]), (ck_hbm, ck_ref), (cv_hbm, cv_ref), (len_hbm, len_ref)))
    ]
    own_copies = [
        pltpu.make_async_copy(
            ref.at[:, pl.ds(pl.multiple_of(at * 128, 128), 128)], dst.at[i], own_sem.at[sem + i]
        )
        for at, dst, sem in ((xh, kvb.at[0, 0], 0), (1 - xh, others, 6))
        for i, ref in enumerate((pk_ref, pv_ref))
    ]
    for c in loads + own_copies:
        c.start()

    barrier = pltpu.get_barrier_semaphore()

    def greet(to):
        pl.semaphore_signal(barrier, inc=1, device_id=to, device_id_type=MESH)

    for e in range(8):
        @pl.when(other(e))
        def _():
            greet(source(e))
            greet(target(e))
    partner = (y * 2 + 1 - xh, z, head)
    greet(partner)
    for s in range(1, n):
        greet(device(u, around(v, s)))
    right, left = device(around(u, 1), v), device(around(u, -1), v)
    greet(right)
    greet(left)
    for s in range(2, near + 1):
        greet(device(around(u, s), v))
        greet(device(around(u, -s), v))

    for c in loads:
        c.wait()
    ends, so_far = [], 0
    for c in range(8):
        so_far = so_far + len_ref[0, c]
        ends.append(so_far)
    place = lax.broadcasted_iota(jnp.int32, (8, 128), 1) + 128 * lax.broadcasted_iota(jnp.int32, (8, 128), 0)
    segment = fold(jnp.add, [jnp.where(end <= place, 1.0, 0.0) for end in ends])
    cks, cvs = ck_ref[...].astype(F32), cv_ref[...].astype(F32)
    for k in range(8):
        stage[0:4] = cks[k * 4 : k * 4 + 4]
        stage[4:8] = cvs[k * 4 : k * 4 + 4]
        stage[8:16] = segment
        outbox[k, 32:48, :] = stage[0:16].astype(BF)

    pl.semaphore_wait(barrier, 1 + (n - 1) + 2 * near + 16 - 2 * here.astype(jnp.int32))

    def remote(src, dst, send, recv, to):
        return pltpu.make_async_remote_copy(
            src_ref=src, dst_ref=dst, send_sem=send, recv_sem=recv, device_id=to, device_id_type=MESH
        )

    def box(e):
        k = 2 * members[e][1] + members[e][0]
        return remote(outbox.at[k], inbox.at[me], box_send.at[e], box_recv.at[me], target(e))

    def box_in(e):
        return remote(outbox.at[0], inbox.at[e], box_send.at[e], box_recv.at[e], source(e))

    for e in range(8):
        @pl.when(other(e))
        def _():
            box(e).start()

        @pl.when(jnp.logical_not(other(e)))
        def _():
            inbox[e] = outbox[kv_head]
    crossing = [remote(others.at[i], kvb.at[0, 1, i], pair_send.at[i], pair_recv.at[i], partner) for i in (0, 1)]

    def kv_copies(s, piece):
        out = []
        sub, i = piece // 2, piece % 2
        for sign, slot, to in ((1, right_slot, right), (-1, functools.partial(left_slot, n), left)):
            if sub == 0:
                hops = [(s - 1, s, 1)]
            elif s == 1:
                hops = [(0, d, d) for d in range(near, 0, -1)]
            else:
                hops = [(near, near + d, d) for d in range(near, 0, -1)]
            for old, new, far in hops:
                if new == half and sub == (sign > 0):
                    continue
                src, dst = slot(old) if old else 0, slot(new)
                out.append(remote(
                    kvb.at[src, sub, i], kvb.at[dst, sub, i], kv_send.at[dst, piece], kv_recv.at[dst, piece], device(around(u, sign * far), v)
                ))
        return out

    def kv_do(s, piece, act):
        if s <= (half if piece < 2 else 2):
            for c in kv_copies(s, piece):
                act(c)

    def kv_event(s, piece):
        kv_do(s, piece, lambda c: c.wait_recv())
        kv_do(s + 1, piece, lambda c: c.start())

    for c in own_copies[2:]:
        c.wait()
    for c in crossing:
        c.start()

    for i in (0, 1):
        own_copies[i].wait()
        kv_do(1, i, lambda c: c.start())

    def q_copies(far):
        out = []
        for s in range(1, near + 1):
            for sign, slot in ((1, right_slot), (-1, functools.partial(left_slot, n))):
                src, dst = (slot(near), slot(near + s)) if far else (0, slot(s))
                last = near + s == half
                rows = pl.ds(0, CHUNK)
                if far and last:
                    rows = pl.ds(0 if sign > 0 else CHUNK // 2, CHUNK // 2)
                sem = n if far and last and sign < 0 else dst
                out.append(remote(
                    qb.at[src, rows], qb.at[dst, rows], q_send.at[sem], q_recv.at[sem], device(u, around(v, sign * s))
                ))
        return out

    def q_do(far, act):
        for c in q_copies(far):
            act(c)

    def scattered():
        for e in range(8):
            @pl.when(other(e))
            def _():
                box_in(e).wait_recv()
        for e in range(8):
            qb[0, e * 32 : e * 32 + 32, :] = inbox[e, 0:32, :]
            extra = inbox[e, 32:48, :].astype(F32)
            stage[e * 4 : e * 4 + 4] = extra[0:4]
            stage[32 + e * 4 : 32 + e * 4 + 4] = extra[4:8]
        qb[0, TILE : TILE + 64, :] = stage[...].astype(BF)
        q_do(False, lambda c: c.start())

    def run(order):
        for token in order:
            if token == "S":
                scattered()
            elif token == "N":
                q_do(False, lambda c: c.wait_recv())
                q_do(True, lambda c: c.start())
            elif token == "F":
                q_do(True, lambda c: c.wait_recv())
            elif token[0] == "X":
                i = int(token[1])
                crossing[i].wait_recv()
                kv_do(1, 2 + i, lambda c: c.start())
            else:
                kv_event(int(token[0]), int(token[1]))

    run(ORDER)

    def own_continuation():
        for r in range(n):
            d = -((r + 1) // 2) if r % 2 else r // 2
            at = pl.ds(pl.multiple_of(around(v, d) * 32, 32), 32)
            ckb[at, :] = qb[r, TILE : TILE + 32, :]
            cvb[at, :] = qb[r, TILE + 32 : TILE + 64, :]
        wide = min(128, 32 * n)
        marks = inbox[0, 32:48, :].astype(F32)
        row = lax.broadcasted_iota(jnp.int32, (TILE, wide), 0)
        slot = v * 32 + (row // 32) * 4 + row % 4
        lane = lax.broadcasted_iota(jnp.int32, (TILE, wide), 1)
        halves = range(32 * n // wide)
        own = fold(jnp.add, [
            jnp.sum(jnp.where(lane + h * wide == slot, marks[8 + h : 9 + h, :wide], 0.0), axis=1, keepdims=True) for h in halves
        ])
        scores = []
        for h in halves:
            allowed = (marks[8 + h : 9 + h, :wide] == own) & (lane + h * wide <= slot)
            scores.append(jnp.where(allowed, dot_nt(qb[0, 0:TILE, :], ckb[h * wide : (h + 1) * wide, :]), MASKED))
        state = (top[0], total[0], mixed[0])
        top[0], total[0], mixed[0] = advance(state, scores, [cvb[h * wide : (h + 1) * wide, :] for h in halves])

    row = lax.broadcasted_iota(jnp.int32, (128, 128), 0)
    lane = lax.broadcasted_iota(jnp.int32, (128, 128), 1)
    diagonal = row == lane

    def finish(r):
        w = jnp.sum(total[r], axis=1, keepdims=True)
        lse = top[r] * SCALE + jnp.log(w)
        for h in range(2):
            lsend[r, h : h + 1, :] = jnp.sum(
                jnp.where(diagonal, lse[h * 128 : h * 128 + 128], 0.0), axis=0, keepdims=True
            )
        return mixed[r] * (1.0 / w)

    def o_copies(r):
        odd = r % 2
        mirror = r + 2 * odd - 1 - r // (n - 1)
        to = device(u, around(v, (1 - odd) * (r // 2) - odd * ((r + 1) // 2)))
        return [
            remote(osend.at[r], orecv.at[mirror], o_send.at[r], o_recv.at[mirror], to),
            remote(lsend.at[r], lrecv.at[mirror], l_send.at[r], l_recv.at[mirror], to),
        ]

    def give(r, _):
        osend[r] = finish(r).astype(BF)
        for c in o_copies(r):
            c.start()
        return 0

    def each_sent(act):
        def one(r, _):
            for c in o_copies(r):
                act(c)
            return 0

        lax.fori_loop(1, n, one, 0)

    pairs, tiles = n // 2, 2 * near + 1
    first = min(FIRST, pairs)
    before = UNITS if n == 8 else {0: ("22", "23")}
    top[...] = jnp.full(top.shape, MASKED, F32)
    total[...] = jnp.zeros(total.shape, F32)
    mixed[...] = jnp.zeros(mixed.shape, F32)

    def unit(low, count, p):
        rows = pl.ds(low, count)
        q = jnp.concatenate([qb[low + r, 0:TILE, :] for r in range(count)], axis=0)
        pieces = [(2 * p + s, ab) for s in (0, 1) for ab in (0, 1)]
        scores = [dot_nt(q, kvb[s, ab, 0]) for s, ab in pieces]
        state = tuple(x[rows].reshape(count * TILE, 128) for x in (top, total, mixed))
        state = advance(state, scores, [kvb[s, ab, 1] for s, ab in pieces])
        for x, new in zip((top, total, mixed), state):
            x[rows] = new.reshape(count, TILE, 128)

    def near_unit(p, _):
        for at, events in before.items():
            @pl.when(p == at)
            def _():
                run(events)

        unit(0, tiles, p)
        return 0

    def far_unit(p, _):
        for at, events in FAR_UNITS.items() if n == 8 else ():
            @pl.when(p == at)
            def _():
                run(events)

        unit(tiles, n - tiles, p)
        return 0

    def give_all(low, high):
        lax.fori_loop(0, high - low, lambda i, c: give(high - 1 - i, c), 0)

    lax.fori_loop(0, first, near_unit, 0)
    if first == pairs:
        give_all(1, tiles)
    run(("F",))
    lax.fori_loop(0, pairs, far_unit, 0)
    give_all(tiles, n)
    if first < pairs:
        lax.fori_loop(first, pairs, near_unit, 0)
        give_all(1, tiles)
    own_continuation()

    def final(e):
        return remote(fsend.at[e * 32 : e * 32 + 32], frecv.at[kv_head], f_send.at[e], f_recv.at[kv_head], source(e))

    def final_in(e):
        k = 2 * members[e][1] + members[e][0]
        return remote(fsend.at[0:32], frecv.at[k], f_send.at[e], f_recv.at[k], target(e))

    def send_back(some):
        for e in some:
            @pl.when(other(e))
            def _():
                final(e).start()

            @pl.when(jnp.logical_not(other(e)))
            def _():
                frecv[kv_head] = fsend[e * 32 : e * 32 + 32, :]

    mine = finish(0)
    each_sent(lambda c: c.wait_recv())
    pieces = [lsend[0, 0:2, :]] + [lrecv[r, 0:2, :] for r in range(1, n)]
    largest = fold(jnp.maximum, pieces)
    shares = [jnp.exp(p - largest) for p in pieces]
    whole = fold(jnp.add, shares)
    shares = [p / whole for p in shares]
    for h in range(2):
        rows = slice(h * 128, h * 128 + 128)
        terms = []
        for r in range(n):
            share = jnp.sum(jnp.where(diagonal, shares[r][h : h + 1, :], 0.0), axis=1, keepdims=True)
            terms.append(share * (mine[rows] if r == 0 else orecv[r, rows, :].astype(F32)))
        fsend[rows, :] = fold(jnp.add, terms).astype(BF)
        send_back(range(h * 4, h * 4 + 4))

    each_sent(lambda c: c.wait_send())
    for c in crossing:
        c.wait_send()
    for s in range(1, half + 1):
        for piece in range(4):
            kv_do(s, piece, lambda c: c.wait_send())
    q_do(False, lambda c: c.wait_send())
    q_do(True, lambda c: c.wait_send())
    for e in range(8):
        @pl.when(other(e))
        def _():
            box(e).wait_send()
            final(e).wait_send()
            final_in(e).wait_recv()
    out_ref[...] = frecv[...]


def by_head(flat, heads):
    return jnp.transpose(flat.reshape(4, 8 * heads, 128), (1, 0, 2)).reshape(-1, 128)


def per_device(n, query, prefix_keys, prefix_value_cache, cont_keys, continuation_values, cont_lengths):
    rows = prefix_keys.shape[0]
    vmem = pl.BlockSpec(memory_space=pltpu.VMEM)
    anywhere = pl.BlockSpec(memory_space=pltpu.MemorySpace.HBM)
    dma = pltpu.SemaphoreType.DMA
    out = pl.pallas_call(
        functools.partial(kernel, n),
        out_shape=jax.ShapeDtypeStruct((8, 32, 128), BF),
        in_specs=[anywhere] * 6,
        out_specs=vmem,
        scratch_shapes=[
            pltpu.VMEM((32, 128), BF),
            pltpu.VMEM((32, 128), BF),
            pltpu.SMEM(cont_lengths.shape, jnp.int32),
            pltpu.VMEM((64, 128), F32),
            pltpu.VMEM((8, 48, 128), BF),
            pltpu.VMEM((8, 48, 128), BF),
            pltpu.VMEM((n, 2, 2, rows, 128), BF),
            pltpu.VMEM((2, rows, 128), BF),
            pltpu.VMEM((n, CHUNK, 128), BF),
            pltpu.VMEM((n, TILE, 128), F32),
            pltpu.VMEM((n, TILE, 128), F32),
            pltpu.VMEM((n, TILE, 128), F32),
            pltpu.VMEM((32 * n, 128), BF),
            pltpu.VMEM((32 * n, 128), BF),
            pltpu.VMEM((n, TILE, 128), BF),
            pltpu.VMEM((n, 8, 128), F32),
            pltpu.VMEM((n, TILE, 128), BF),
            pltpu.VMEM((n, 8, 128), F32),
            pltpu.VMEM((TILE, 128), BF),
            pltpu.VMEM((8, 32, 128), BF),
            dma((8,)), dma((8,)), dma((8,)), dma((2,)), dma((2,)), dma((n, 4)), dma((n, 4)),
            dma((n + 1,)), dma((n + 1,)), dma((n,)), dma((n,)), dma((n,)), dma((n,)), dma((8,)), dma((8,)),
        ],
        compiler_params=pltpu.CompilerParams(
            collective_id=0, has_side_effects=True, vmem_limit_bytes=40 * 1024 * 1024
        ),
        cost_estimate=pl.CostEstimate(flops=4_300_000_000, bytes_accessed=1_000_000, transcendentals=8_400_000),
    )(*[
        pltpu.with_memory_space_constraint(x, pltpu.MemorySpace.HBM)
        for x in (
            by_head(query, 8).reshape(8, 32, 128), by_head(cont_keys, 1), by_head(continuation_values, 1),
            cont_lengths, prefix_keys, prefix_value_cache,
        )
    ])
    return jnp.transpose(out.reshape(8, 8, 4, 128), (2, 0, 1, 3)).reshape(query.shape)


def solution(mesh):
    n = mesh.shape["cand"]
    return jax.shard_map(
        functools.partial(per_device, n),
        mesh=mesh,
        in_specs=(
            P("cand", ("ctx", "head"), None),
            P(("ctx", "cand"), "head"),
            P(("ctx", "cand"), "head"),
            P("cand", ("ctx", "head"), None),
            P("cand", ("ctx", "head"), None),
            P("cand", None),
        ),
        out_specs=P("cand", ("ctx", "head"), None),
        check_vma=False,
    )
```

```python
import functools
import math

import jax
import jax.numpy as jnp
from jax import lax
from jax.experimental import pallas as pl
from jax.experimental.pallas import tpu as pltpu
from jax.sharding import PartitionSpec as P

MESH = pl.DeviceIdType.MESH
BF = jnp.bfloat16
F32 = jnp.float32
HEAD_SIZE = 128
SCALE = HEAD_SIZE ** -0.5
EXP2_SCALE = SCALE * math.log2(math.e)
TILE = 256
CHUNK = TILE + 64
MASKED = -1e30


def dot_nt(a, b):
    return lax.dot_general(a, b, (((1,), (1,)), ((), ())), preferred_element_type=F32)


def lanes(parts):
    return [p[:, i : i + 128] for p in parts for i in range(0, p.shape[1], 128)]


def fold(op, parts):
    parts = list(parts)
    while len(parts) > 1:
        pairs = [op(a, b) for a, b in zip(parts[::2], parts[1::2])]
        parts = pairs + (parts[-1:] if len(parts) % 2 else [])
    return parts[0]


def advance(state, scores, values):
    top = jnp.max(fold(jnp.maximum, lanes(scores)), axis=1, keepdims=True)
    if state is None:
        top = jnp.broadcast_to(top, (top.shape[0], 128))
    else:
        old = state[0]
        top = jnp.maximum(old, top)
        fade = jnp.exp2((old - top) * EXP2_SCALE)
    weights = [
        [jnp.exp2((s - top) * EXP2_SCALE) for s in lanes([part])] for part in scores
    ]
    total = fold(jnp.add, [w for part in weights for w in part])
    mixed = fold(
        jnp.add,
        [
            jnp.dot(jnp.concatenate([w.astype(BF) for w in part], axis=1), v, preferred_element_type=F32)
            for part, v in zip(weights, values)
        ],
    )
    if state is not None:
        total = total + fade * state[1]
        mixed = mixed + fade * state[2]
    return top, total, mixed


def right_slot(s):
    return 2 * s - 1 if s else 0


def left_slot(n, s):
    return 2 * s if s < n // 2 else n - 1


def place_of(n, slot, sub):
    if slot in (0, n - 1):
        return 2 * slot + sub
    return 4 * ((slot + 1) // 2) - 2 + 2 * sub + (slot + 1) % 2


ORDER = ("S", "10", "11", "X0", "X1", "N", "20", "21", "12", "13",)
UNITS = {1: ("30", "31",)}
FIRST = 2
FAR_UNITS = {3: ("22", "23", "40", "41",)}


def kernel(
    n, q_hbm, ck_hbm, cv_hbm, len_hbm, pk_ref, pv_ref, out_ref,
    ck_ref, cv_ref, len_ref,
    stage, outbox, inbox, kvb, others, qb, top, total, mixed, ckb, cvb,
    osend, lsend, orecv, lrecv, fsend, frecv,
    own_sem, box_send, box_recv, pair_send, pair_recv, kv_send, kv_recv,
    q_send, q_recv, o_send, o_recv, l_send, l_recv, f_send, f_recv,
):
    half, near = n // 2, n // 4
    ctx, z, head = lax.axis_index("ctx"), lax.axis_index("cand"), lax.axis_index("head")
    y, xh, core = ctx // 2, ctx % 2, head % 2
    me = xh * 4 + head
    kv_head = 2 * head + xh

    def around(a, s):
        return lax.rem(a + s + n, n)

    u = z + core * (y - z)
    v = y + core * (around(z, -half) - y)

    def device(uu, vv):
        return ((vv + core * (uu - vv)) * 2 + xh, uu + core * (around(vv, half) - uu), head)

    members = [(e // 4, e % 4) for e in range(8)]
    here = core == 0

    def source(e):
        return (v * 2 + members[e][0], u, members[e][1])

    def target(e):
        return (y * 2 + members[e][0], z, members[e][1]) if e % 2 == 0 else (z * 2 + members[e][0], around(y, half), members[e][1])

    def other(e):
        return jnp.logical_not((me == e) & here)

    loads = [
        pltpu.make_async_copy(src, dst, own_sem.at[2 + i])
        for i, (src, dst) in enumerate(((q_hbm, outbox.at[:, 0:32]), (ck_hbm, ck_ref), (cv_hbm, cv_ref), (len_hbm, len_ref)))
    ]
    own_copies = [
        pltpu.make_async_copy(
            ref.at[:, pl.ds(pl.multiple_of(at * 128, 128), 128)], dst.at[i], own_sem.at[sem + i]
        )
        for at, dst, sem in ((xh, kvb.at[0], 0), (1 - xh, others, 6))
        for i, ref in enumerate((pk_ref, pv_ref))
    ]
    for c in loads + own_copies:
        c.start()

    barrier = pltpu.get_barrier_semaphore()

    def greet(to):
        pl.semaphore_signal(barrier, inc=1, device_id=to, device_id_type=MESH)

    for e in range(8):
        @pl.when(other(e))
        def _():
            greet(source(e))
    partner = (y * 2 + 1 - xh, z, head)
    greet(partner)
    for s in range(1, near + 1):
        greet(device(u, around(v, s)))
        greet(device(u, around(v, -s)))
    right, left = device(around(u, 1), v), device(around(u, -1), v)
    greet(right)
    greet(left)
    for s in range(2, near + 1):
        greet(device(around(u, s), v))
        greet(device(around(u, -s), v))

    for c in loads:
        c.wait()
    ends, so_far = [], 0
    for c in range(8):
        so_far = so_far + len_ref[0, c]
        ends.append(so_far)
    place = lax.broadcasted_iota(jnp.int32, (8, 128), 1) + 128 * lax.broadcasted_iota(jnp.int32, (8, 128), 0)
    segment = fold(jnp.add, [jnp.where(end <= place, 1.0, 0.0) for end in ends])
    cks, cvs = ck_ref[...].astype(F32), cv_ref[...].astype(F32)
    for k in range(8):
        stage[0:4] = cks[k * 4 : k * 4 + 4]
        stage[4:8] = cvs[k * 4 : k * 4 + 4]
        stage[8:16] = segment
        outbox[k, 32:48, :] = stage[0:16].astype(BF)

    top[...] = jnp.full(top.shape, MASKED, F32)
    total[...] = jnp.zeros(total.shape, F32)
    mixed[...] = jnp.zeros(mixed.shape, F32)

    pl.semaphore_wait(barrier, 1 + 4 * near + 8 - here.astype(jnp.int32))

    def remote(src, dst, send, recv, to):
        return pltpu.make_async_remote_copy(
            src_ref=src, dst_ref=dst, send_sem=send, recv_sem=recv, device_id=to, device_id_type=MESH
        )

    def box(e):
        k = 2 * members[e][1] + members[e][0]
        return remote(outbox.at[k], inbox.at[me], box_send.at[e], box_recv.at[me], target(e))

    def box_in(e):
        return remote(outbox.at[0], inbox.at[e], box_send.at[e], box_recv.at[e], source(e))

    for e in range(8):
        @pl.when(other(e))
        def _():
            box(e).start()

        @pl.when(jnp.logical_not(other(e)))
        def _():
            inbox[e] = outbox[kv_head]
    crossing = [remote(others.at[i], kvb.at[1, i], pair_send.at[i], pair_recv.at[i], partner) for i in (0, 1)]

    def kv_copies(s, piece):
        out = []
        sub, i = piece // 2, piece % 2
        for sign, slot, to in ((1, right_slot, right), (-1, functools.partial(left_slot, n), left)):
            if sub == 0:
                hops = [(s - 1, s, 1)]
            elif s == 1:
                hops = [(0, d, d) for d in range(near, 0, -1)]
            else:
                hops = [(near, near + d, d) for d in range(near, 0, -1)]
            for old, new, far in hops:
                if new == half and sub == (sign > 0):
                    continue
                src, dst = slot(old) if old else 0, slot(new)
                out.append(remote(
                    kvb.at[place_of(n, src, sub), i], kvb.at[place_of(n, dst, sub), i], kv_send.at[dst, piece], kv_recv.at[dst, piece], device(around(u, sign * far), v)
                ))
        return out

    def kv_do(s, piece, act):
        if s <= (half if piece < 2 else 2):
            for c in kv_copies(s, piece):
                act(c)

    def kv_event(s, piece):
        kv_do(s, piece, lambda c: c.wait_recv())
        kv_do(s + 1, piece, lambda c: c.start())

    for c in own_copies[2:]:
        c.wait()
    for c in crossing:
        c.start()

    for i in (0, 1):
        own_copies[i].wait()
        kv_do(1, i, lambda c: c.start())

    def q_copies(far):
        out = []
        for s in range(1, near + 1):
            for sign, slot in ((1, right_slot), (-1, functools.partial(left_slot, n))):
                src, dst = (slot(near), slot(near + s)) if far else (0, slot(s))
                last = near + s == half
                rows = pl.ds(0, CHUNK)
                if far and last:
                    rows = pl.ds(0 if sign > 0 else CHUNK // 2, CHUNK // 2)
                sem = n if far and last and sign < 0 else dst
                out.append(remote(
                    qb.at[src, rows], qb.at[dst, rows], q_send.at[sem], q_recv.at[sem], device(u, around(v, sign * s))
                ))
        return out

    def q_do(far, act):
        for c in q_copies(far):
            act(c)

    def scattered():
        for e in range(8):
            @pl.when(other(e))
            def _():
                box_in(e).wait_recv()
        for e in range(8):
            qb[0, e * 32 : e * 32 + 32, :] = inbox[e, 0:32, :]
            extra = inbox[e, 32:48, :].astype(F32)
            stage[e * 4 : e * 4 + 4] = extra[0:4]
            stage[32 + e * 4 : 32 + e * 4 + 4] = extra[4:8]
        qb[0, TILE : TILE + 64, :] = stage[...].astype(BF)
        q_do(False, lambda c: c.start())

    def unit(low, count, p):
        rows = pl.ds(low, count)
        q = jnp.concatenate([qb[low + r, 0:TILE, :] for r in range(count)], axis=0)
        scores = [dot_nt(q, kvb[4 * p + i, 0]) for i in range(4)]
        state = tuple(x[rows].reshape(count * TILE, 128) for x in (top, total, mixed))
        state = advance(state, scores, [kvb[4 * p + i, 1] for i in range(4)])
        for x, new in zip((top, total, mixed), state):
            x[rows] = new.reshape(count, TILE, 128)

    def own_unit(p, _):
        unit(0, 1, p)
        return 0

    def run(order):
        for token in order:
            if token == "S":
                scattered()
            elif token == "N":
                q_do(False, lambda c: c.wait_recv())
                q_do(True, lambda c: c.start())
            elif token == "O":
                own_unit(0, 0)
            elif token == "F":
                q_do(True, lambda c: c.wait_recv())
            elif token[0] == "X":
                i = int(token[1])
                crossing[i].wait_recv()
                kv_do(1, 2 + i, lambda c: c.start())
            else:
                kv_event(int(token[0]), int(token[1]))

    run(ORDER)

    def own_continuation():
        for r in range(n):
            d = -((r + 1) // 2) if r % 2 else r // 2
            at = pl.ds(pl.multiple_of(around(v, d) * 32, 32), 32)
            ckb[at, :] = qb[r, TILE : TILE + 32, :]
            cvb[at, :] = qb[r, TILE + 32 : TILE + 64, :]
        wide = min(128, 32 * n)
        marks = inbox[0, 32:48, :].astype(F32)
        row = lax.broadcasted_iota(jnp.int32, (TILE, wide), 0)
        slot = v * 32 + (row // 32) * 4 + row % 4
        lane = lax.broadcasted_iota(jnp.int32, (TILE, wide), 1)
        halves = range(32 * n // wide)
        own = fold(jnp.add, [
            jnp.sum(jnp.where(lane + h * wide == slot, marks[8 + h : 9 + h, :wide], 0.0), axis=1, keepdims=True) for h in halves
        ])
        scores = []
        for h in halves:
            allowed = (marks[8 + h : 9 + h, :wide] == own) & (lane + h * wide <= slot)
            scores.append(jnp.where(allowed, dot_nt(qb[0, 0:TILE, :], ckb[h * wide : (h + 1) * wide, :]), MASKED))
        state = (top[0], total[0], mixed[0])
        top[0], total[0], mixed[0] = advance(state, scores, [cvb[h * wide : (h + 1) * wide, :] for h in halves])

    row = lax.broadcasted_iota(jnp.int32, (128, 128), 0)
    lane = lax.broadcasted_iota(jnp.int32, (128, 128), 1)
    diagonal = row == lane

    def finish(r):
        w = jnp.sum(total[r], axis=1, keepdims=True)
        lse = top[r] * SCALE + jnp.log(w)
        for h in range(2):
            lsend[r, h : h + 1, :] = jnp.sum(
                jnp.where(diagonal, lse[h * 128 : h * 128 + 128], 0.0), axis=0, keepdims=True
            )
        return mixed[r] * (1.0 / w)

    def o_copies(r):
        odd = r % 2
        mirror = r + 2 * odd - 1 - r // (n - 1)
        to = device(u, around(v, (1 - odd) * (r // 2) - odd * ((r + 1) // 2)))
        return [
            remote(osend.at[r], orecv.at[mirror], o_send.at[r], o_recv.at[mirror], to),
            remote(lsend.at[r], lrecv.at[mirror], l_send.at[r], l_recv.at[mirror], to),
        ]

    def give(r, _):
        osend[r] = finish(r).astype(BF)
        for c in o_copies(r):
            c.start()
        return 0

    def each_sent(act):
        def one(r, _):
            for c in o_copies(r):
                act(c)
            return 0

        lax.fori_loop(1, n, one, 0)

    pairs, tiles = n // 2, 2 * near + 1
    first = min(FIRST, pairs)
    before = UNITS if n == 8 else {0: ("22", "23")}
    def near_unit(p, _):
        for at, events in before.items():
            @pl.when(p == at)
            def _():
                run(events)

        unit(1, tiles - 1, p)
        return 0

    def far_unit(p, _):
        for at, events in FAR_UNITS.items() if n == 8 else ():
            @pl.when(p == at)
            def _():
                run(events)

        unit(tiles, n - tiles, p)
        return 0

    def give_all(low, high):
        lax.fori_loop(0, high - low, lambda i, c: give(high - 1 - i, c), 0)

    lax.fori_loop(0, first, near_unit, 0)
    if first == pairs:
        give_all(1, tiles)
    run(("F",))
    lax.fori_loop(0, pairs, far_unit, 0)
    give_all(tiles, n)
    if first < pairs:
        lax.fori_loop(first, pairs, near_unit, 0)
        give_all(1, tiles)
    lax.fori_loop(0, pairs, own_unit, 0)
    own_continuation()

    def final(e):
        return remote(fsend.at[e * 32 : e * 32 + 32], frecv.at[kv_head], f_send.at[e], f_recv.at[kv_head], source(e))

    def final_in(e):
        k = 2 * members[e][1] + members[e][0]
        return remote(fsend.at[0:32], frecv.at[k], f_send.at[e], f_recv.at[k], target(e))

    def send_back(some):
        for e in some:
            @pl.when(other(e))
            def _():
                final(e).start()

            @pl.when(jnp.logical_not(other(e)))
            def _():
                frecv[kv_head] = fsend[e * 32 : e * 32 + 32, :]

    mine = finish(0)
    each_sent(lambda c: c.wait_recv())
    pieces = [lsend[0, 0:2, :]] + [lrecv[r, 0:2, :] for r in range(1, n)]
    largest = fold(jnp.maximum, pieces)
    shares = [jnp.exp(p - largest) for p in pieces]
    whole = fold(jnp.add, shares)
    shares = [p / whole for p in shares]
    for h in range(2):
        rows = slice(h * 128, h * 128 + 128)
        terms = []
        for r in range(n):
            share = jnp.sum(jnp.where(diagonal, shares[r][h : h + 1, :], 0.0), axis=1, keepdims=True)
            terms.append(share * (mine[rows] if r == 0 else orecv[r, rows, :].astype(F32)))
        fsend[rows, :] = fold(jnp.add, terms).astype(BF)
        send_back(range(h * 4, h * 4 + 4))

    each_sent(lambda c: c.wait_send())
    for c in crossing:
        c.wait_send()
    for s in range(1, half + 1):
        for piece in range(4):
            kv_do(s, piece, lambda c: c.wait_send())
    q_do(False, lambda c: c.wait_send())
    q_do(True, lambda c: c.wait_send())
    for e in range(8):
        @pl.when(other(e))
        def _():
            box(e).wait_send()
            final(e).wait_send()
            final_in(e).wait_recv()
    out_ref[...] = frecv[...]


def by_head(flat, heads):
    return jnp.transpose(flat.reshape(4, 8 * heads, 128), (1, 0, 2)).reshape(-1, 128)


def per_device(n, query, prefix_keys, prefix_value_cache, cont_keys, continuation_values, cont_lengths):
    rows = prefix_keys.shape[0]
    vmem = pl.BlockSpec(memory_space=pltpu.VMEM)
    anywhere = pl.BlockSpec(memory_space=pltpu.MemorySpace.HBM)
    dma = pltpu.SemaphoreType.DMA
    out = pl.pallas_call(
        functools.partial(kernel, n),
        out_shape=jax.ShapeDtypeStruct((8, 32, 128), BF),
        in_specs=[anywhere] * 6,
        out_specs=vmem,
        scratch_shapes=[
            pltpu.VMEM((32, 128), BF),
            pltpu.VMEM((32, 128), BF),
            pltpu.SMEM(cont_lengths.shape, jnp.int32),
            pltpu.VMEM((64, 128), F32),
            pltpu.VMEM((8, 48, 128), BF),
            pltpu.VMEM((8, 48, 128), BF),
            pltpu.VMEM((2 * n, 2, rows, 128), BF),
            pltpu.VMEM((2, rows, 128), BF),
            pltpu.VMEM((n, CHUNK, 128), BF),
            pltpu.VMEM((n, TILE, 128), F32),
            pltpu.VMEM((n, TILE, 128), F32),
            pltpu.VMEM((n, TILE, 128), F32),
            pltpu.VMEM((32 * n, 128), BF),
            pltpu.VMEM((32 * n, 128), BF),
            pltpu.VMEM((n, TILE, 128), BF),
            pltpu.VMEM((n, 8, 128), F32),
            pltpu.VMEM((n, TILE, 128), BF),
            pltpu.VMEM((n, 8, 128), F32),
            pltpu.VMEM((TILE, 128), BF),
            pltpu.VMEM((8, 32, 128), BF),
            dma((8,)), dma((8,)), dma((8,)), dma((2,)), dma((2,)), dma((n, 4)), dma((n, 4)),
            dma((n + 1,)), dma((n + 1,)), dma((n,)), dma((n,)), dma((n,)), dma((n,)), dma((8,)), dma((8,)),
        ],
        compiler_params=pltpu.CompilerParams(
            collective_id=0, has_side_effects=True, vmem_limit_bytes=40 * 1024 * 1024
        ),
        cost_estimate=pl.CostEstimate(flops=4_300_000_000, bytes_accessed=1_000_000, transcendentals=8_400_000),
    )(*[
        pltpu.with_memory_space_constraint(x, pltpu.MemorySpace.HBM)
        for x in (
            by_head(query, 8).reshape(8, 32, 128), by_head(cont_keys, 1), by_head(continuation_values, 1),
            cont_lengths, prefix_keys, prefix_value_cache,
        )
    ])
    return jnp.transpose(out.reshape(8, 8, 4, 128), (2, 0, 1, 3)).reshape(query.shape)


def solution(mesh):
    n = mesh.shape["cand"]
    return jax.shard_map(
        functools.partial(per_device, n),
        mesh=mesh,
        in_specs=(
            P("cand", ("ctx", "head"), None),
            P(("ctx", "cand"), "head"),
            P(("ctx", "cand"), "head"),
            P("cand", ("ctx", "head"), None),
            P("cand", ("ctx", "head"), None),
            P("cand", None),
        ),
        out_specs=P("cand", ("ctx", "head"), None),
        check_vma=False,
    )
```
